32 devices in a mesh: fsdp: 4 (over y, core), ctx: 4 (over z), tp: 2 (over x).
Axes of the slice: x: 2, y: 2, z: 4, core: 2. Of those that a mesh axis runs over, the one named last changes fastest.
Arguments:
- tokens: bfloat16 [4, 2048, 1024], P('fsdp', 'ctx'), may hold values from -6 to 6
- lengths: int32 [4, 6], P('fsdp'), may hold values from 1 to 1536, as said below
- query_weight: bfloat16 [1024, 1024], P('fsdp', 'tp'), may hold values from -0.1875 to 0.1875
- key_weight: bfloat16 [1024, 512], P('fsdp', 'tp'), may hold values from -0.1875 to 0.1875
- value_weight: bfloat16 [1024, 512], P('fsdp', 'tp'), may hold values from -0.1875 to 0.1875
- out_weight: bfloat16 [1024, 1024], P('tp', 'fsdp'), may hold values from -0.75 to 0.75
- gate_weight: bfloat16 [1024, 4608], P('fsdp', 'tp'), may hold values from -0.1875 to 0.1875
- up_weight: bfloat16 [1024, 4608], P('fsdp', 'tp'), may hold values from -0.1875 to 0.1875
- down_weight: bfloat16 [4608, 1024], P('tp', 'fsdp'), may hold values from -0.09375 to 0.09375
- attn_gain: float32 [1024], replicated, may hold values from 0.5 to 1.5
- ffn_gain: float32 [1024], replicated, may hold values from 0.5 to 1.5
- query_gain: float32 [64], replicated, may hold values from 0.5 to 1.5
- key_gain: float32 [64], replicated, may hold values from 0.5 to 1.5
- out_grad: bfloat16 [4, 2048, 1024], P('fsdp', 'ctx'), may hold values from -6 to 6
Outputs:
- mixed: bfloat16 [4, 2048, 1024], P('fsdp', 'ctx')
- tokens_grad: float32 [4, 2048, 1024], P('fsdp', 'ctx')
- grad_query: float32 [1024, 1024], P('fsdp', 'tp')
- grad_key: float32 [1024, 512], P('fsdp', 'tp')
- grad_value: float32 [1024, 512], P('fsdp', 'tp')
- grad_out: float32 [1024, 1024], P('tp', 'fsdp')
- grad_gate: float32 [1024, 4608], P('fsdp', 'tp')
- grad_up: float32 [1024, 4608], P('fsdp', 'tp')
- grad_down: float32 [4608, 1024], P('tp', 'fsdp')
- grad_attn_gain: float32 [1024], replicated
- grad_ffn_gain: float32 [1024], replicated
- grad_query_gain: float32 [64], replicated
- grad_key_gain: float32 [64], replicated
The draws below stay inside these ranges and needn't reach their ends.
Inputs may be any that keep to these rules, and one draw needn't show every extreme that they name: `lengths`: each row sums to 2048; in each row the longest sequence has exactly 1536 tokens.
All inputs are finite; a program needn't handle non-finite values.
Results may differ from the reference program's by a relative error of at most 0.019.
Values may be sent and summed in bfloat16 or wider, within the bound.
A program may use at most 192 MiB of HBM per device.

```python
import jax
import jax.numpy as jnp
from jax import lax

D = 1024
H = 16
KV = 8
HD = 64
FF = 4608
SLICE_TOK = 512
PACK_LEN = 2048
PACK_ROWS = 4


def draw_lengths(key, part):
    key = jax.random.fold_in(key, 11)
    subkeys = jax.random.split(key, 4)
    leading = jax.random.randint(subkeys[0], (PACK_ROWS,), 2, SLICE_TOK - 2)
    trailing = SLICE_TOK - leading
    first_cut = jax.random.randint(subkeys[1], (PACK_ROWS,), 1, leading)
    last_cut = jax.random.randint(subkeys[2], (PACK_ROWS,), 1, trailing - 1)
    remaining = trailing - last_cut
    middle_cut = jax.random.randint(subkeys[3], (PACK_ROWS,), 1, remaining)
    longest = jnp.full((PACK_ROWS,), PACK_LEN - SLICE_TOK, jnp.int32)
    return jnp.stack([first_cut, leading - first_cut, longest, last_cut, middle_cut, remaining - middle_cut], axis=1).astype(jnp.int32)


def block_scale(stream_key, extent, cuts, low, largest):
    loudness = 1.0
    for position, parts in cuts:
        steps = jax.random.uniform(jax.random.fold_in(jax.random.fold_in(stream_key, 6), position), (parts,), jnp.float32, low / len(cuts), largest / len(cuts))
        loudness = loudness * jnp.repeat(jnp.exp(steps), extent[position] // parts).reshape((-1,) + (1,) * (len(extent) - 1 - position))
    return loudness


def normal_values(rng, shape, spread, bound, cuts=(), kind=jnp.bfloat16):
    result = spread * jax.random.normal(rng, shape, jnp.float32)
    if cuts:
        result = result * block_scale(rng, shape, cuts, -0.22, 0.18)
    return jnp.clip(result, -bound, bound).astype(kind)


def setup_inputs(seed: int = 0) -> dict:
    key_list = jax.random.split(jax.random.key(seed), 15)
    tokens = normal_values(key_list[0], (PACK_ROWS, PACK_LEN, D), 1.0, 6.0, ((0, 4), (1, 4)))
    lengths = draw_lengths(jax.random.fold_in(key_list[14], 71), 0)
    query_weight = normal_values(key_list[2], (D, H * HD), D ** -0.5, 0.1875, ((0, 4), (1, 2)))
    key_weight = normal_values(key_list[3], (D, KV * HD), D ** -0.5, 0.1875, ((0, 4), (1, 2)))
    value_weight = normal_values(key_list[4], (D, KV * HD), D ** -0.5, 0.1875, ((0, 4), (1, 2)))
    out_weight = normal_values(key_list[5], (H * HD, D), HD ** -0.5, 0.75, ((0, 2), (1, 4)))
    gate_weight = normal_values(key_list[6], (D, FF), D ** -0.5, 0.1875, ((0, 4), (1, 2)))
    up_weight = normal_values(key_list[7], (D, FF), D ** -0.5, 0.1875, ((0, 4), (1, 2)))
    down_weight = normal_values(key_list[8], (FF, D), FF ** -0.5, 0.09375, ((0, 2), (1, 4)))
    attn_gain = jnp.clip(1.0 + 0.1 * jax.random.normal(key_list[9], (D,), jnp.float32), 0.5, 1.5)
    ffn_gain = jnp.clip(1.0 + 0.1 * jax.random.normal(key_list[10], (D,), jnp.float32), 0.5, 1.5)
    query_gain = jnp.clip(1.0 + 0.1 * jax.random.normal(key_list[11], (HD,), jnp.float32), 0.5, 1.5)
    key_gain = jnp.clip(1.0 + 0.1 * jax.random.normal(key_list[12], (HD,), jnp.float32), 0.5, 1.5)
    out_grad = normal_values(key_list[13], (PACK_ROWS, PACK_LEN, D), 1.0, 6.0, ((0, 4), (1, 4)))
    return dict(tokens=tokens, lengths=lengths, query_weight=query_weight, key_weight=key_weight, value_weight=value_weight, out_weight=out_weight, gate_weight=gate_weight, up_weight=up_weight, down_weight=down_weight, attn_gain=attn_gain, ffn_gain=ffn_gain, query_gain=query_gain, key_gain=key_gain, out_grad=out_grad)


@jax.custom_vjp
def low(v):
    return lax.optimization_barrier(v.astype(jnp.bfloat16)).astype(jnp.float32)

@jax.custom_vjp
def low_back(v):
    return v

def low_keep(v):
    return (low(v), None)

def low_pass(kept, grad):
    return (grad,)

def back_keep(v):
    return (v, None)

def back_low(kept, grad):
    return (low(grad),)
low.defvjp(low_keep, low_pass)
low_back.defvjp(back_keep, back_low)
EPSILON = 1e-05
ROPE_BASE = 1000000.0
exact_mode = lax.Precision.HIGHEST

def matmul(left, right):
    return jnp.dot(left, right, precision=exact_mode, preferred_element_type=jnp.float32)

def rms_norm(values, gain_vec):
    return values * lax.rsqrt(lax.optimization_barrier(jnp.mean(values * values, axis=-1, keepdims=True)) + EPSILON) * gain_vec

def rotate(values, rope_pos):
    half_dim = HD // 2
    frequency = ROPE_BASE ** (-2.0 * jnp.arange(half_dim, dtype=jnp.float32) / HD)
    angles = rope_pos[..., None, None] * frequency
    cosine = jnp.cos(angles)
    sine_part = jnp.sin(angles)
    lower_half = values[..., :half_dim]
    upper_half = values[..., half_dim:]
    return jnp.concatenate([lower_half * cosine - upper_half * sine_part, upper_half * cosine + lower_half * sine_part], axis=-1)

def head_prep(projected, gain_vec, rope_pos):
    shaped = projected.reshape(projected.shape[:-1] + (-1, HD))
    return rotate(rms_norm(shaped, gain_vec), rope_pos)

def pack_forward(inputs, lengths, params):
    query_weight, key_weight, value_weight, out_weight, gate_weight, up_weight, down_weight, attn_gain, ffn_gain, query_gain, key_gain = params
    seq_ends = jnp.cumsum(lengths)
    positions = jnp.arange(PACK_LEN, dtype=jnp.int32)
    passed = (positions[:, None] >= seq_ends[None, :]).astype(jnp.int32)
    seq_start = lax.optimization_barrier(jnp.sum(passed * lengths[None, :], axis=1)).astype(jnp.int32)
    rope_pos = (positions - seq_start).astype(jnp.float32)
    normed = low(rms_norm(inputs, attn_gain))
    queries = low_back(low(head_prep(low_back(matmul(normed, query_weight)), query_gain, rope_pos)))
    keys_rot = low_back(low(head_prep(low_back(matmul(normed, key_weight)), key_gain, rope_pos)))
    values_low = low_back(low(matmul(normed, value_weight))).reshape(PACK_LEN, KV, HD)
    grouped = queries.reshape(PACK_LEN, KV, H // KV, HD)
    row_block = min(512, PACK_LEN)

    def attend(block_index):
        row_start = block_index * row_block
        query_rows = lax.dynamic_slice_in_dim(grouped, row_start, row_block, 0)
        start_rows = lax.dynamic_slice_in_dim(seq_start, row_start, row_block, 0)
        place_rows = lax.dynamic_slice_in_dim(positions, row_start, row_block, 0)
        scores = jnp.einsum('qkgd,tkd->kgqt', query_rows, keys_rot, precision=exact_mode) * HD ** (-0.5)
        scores = low_back(scores)
        visible = (positions[None, :] >= start_rows[:, None]) & (positions[None, :] <= place_rows[:, None])
        scores = jnp.where(visible[None, None], scores, -1e+30)
        row_max = lax.optimization_barrier(jnp.max(scores, axis=-1, keepdims=True))
        exponent = jnp.exp(scores - row_max)
        weights_soft = exponent / lax.optimization_barrier(jnp.sum(exponent, axis=-1, keepdims=True))
        return jnp.einsum('kgqt,tkd->qkgd', low(weights_soft), values_low, precision=exact_mode)
    attended = lax.map(jax.checkpoint(attend), jnp.arange(PACK_LEN // row_block, dtype=jnp.int32))
    attended = low_back(low(attended.reshape(PACK_LEN, H * HD)))
    after_attn = inputs + low_back(matmul(attended, out_weight))
    normed_ffn = low(rms_norm(after_attn, ffn_gain))
    gate_proj = low_back(matmul(normed_ffn, gate_weight))
    up_proj = low_back(matmul(normed_ffn, up_weight))
    hidden = low(jax.nn.silu(gate_proj) * up_proj)
    return after_attn + matmul(hidden, down_weight)

def reference(tokens, lengths, query_weight, key_weight, value_weight, out_weight, gate_weight, up_weight, down_weight, attn_gain, ffn_gain, query_gain, key_gain, out_grad):
    params = tuple((weight.astype(jnp.float32) for weight in (query_weight, key_weight, value_weight, out_weight, gate_weight, up_weight, down_weight, attn_gain, ffn_gain, query_gain, key_gain)))

    def forward(inputs, weights):

        def one_pack(pack_pair):
            return pack_forward(pack_pair[0], pack_pair[1], weights)
        return lax.map(jax.checkpoint(one_pack), (inputs, lengths))
    mixed, pullback = jax.vjp(forward, tokens.astype(jnp.float32), params)
    grad_tokens, grads = pullback(out_grad.astype(jnp.float32))
    return (mixed.astype(jnp.bfloat16), grad_tokens, grads[0], grads[1], grads[2], grads[3], grads[4], grads[5], grads[6], grads[7], grads[8], grads[9], grads[10])
```

```python
import jax
import jax.numpy as jnp
from jax import lax
from jax.experimental import pallas as pl
from jax.experimental.pallas import tpu as pltpu
from jax.sharding import PartitionSpec as P

HD = 64


EPSILON = 1e-05
ROPE_BASE = 1000000.0


def rms_norm(values, gain_vec):
    return (
        values * lax.rsqrt(jnp.mean(values * values, axis=-1, keepdims=True) + EPSILON) * gain_vec
    )


def rotate(values, rope_pos):
    half_dim = HD // 2
    frequency = ROPE_BASE ** (-2.0 * jnp.arange(half_dim, dtype=jnp.float32) / HD)
    angles = rope_pos[..., None, None] * frequency
    cosine = jnp.cos(angles)
    sine_part = jnp.sin(angles)
    lower_half = values[..., :half_dim]
    upper_half = values[..., half_dim:]
    return jnp.concatenate(
        [
            lower_half * cosine - upper_half * sine_part,
            upper_half * cosine + lower_half * sine_part,
        ],
        axis=-1,
    )


def head_prep(projected, gain_vec, rope_pos):
    shaped = projected.reshape(projected.shape[:-1] + (-1, HD))
    return rotate(rms_norm(shaped, gain_vec), rope_pos)


def pairs(axis, step):
    return [(i, i ^ step) for i in range(lax.axis_size(axis))]


def keep_low(values):
    return lax.optimization_barrier(values.astype(jnp.bfloat16))


def both(values):
    total = keep_low(values)
    step = 1
    while step < lax.axis_size("tp"):
        other = lax.ppermute(total, "tp", pairs("tp", step))
        total = total.astype(jnp.float32) + other.astype(jnp.float32)
        step *= 2
        if step < lax.axis_size("tp"):
            total = keep_low(total)
    return total.astype(jnp.float32)


def gather(shard, axis):
    count = lax.axis_size("fsdp")
    mine = lax.axis_index("fsdp")
    pieces = {0: shard}
    step = count // 2
    while step >= 1:
        moved = {
            p ^ step: lax.ppermute(piece, "fsdp", pairs("fsdp", step))
            for p, piece in pieces.items()
        }
        pieces.update(moved)
        step //= 2
    extent = shard.shape[axis]
    reps = [1, 1]
    reps[axis] = count
    full = jnp.tile(shard, reps)
    for p, piece in pieces.items():
        if p:
            full = lax.dynamic_update_slice_in_dim(full, piece, (mine ^ p) * extent, axis)
    return full


def reduce_blocks(block_of):
    count = lax.axis_size("fsdp")
    mine = lax.axis_index("fsdp")
    held = {}
    for p in sorted(range(count), key=lambda p: -(p & 1)):
        held[p] = block_of(mine ^ p)
    step = 1
    while step < count:
        sent = {
            p: lax.ppermute(block.astype(jnp.bfloat16), "fsdp", pairs("fsdp", step))
            for p, block in held.items()
            if p & step
        }
        held = {
            p: block + sent[p ^ step].astype(jnp.float32)
            for p, block in held.items()
            if not p & step
        }
        step *= 2
    return held[0]


def over_ctx(block):
    count = lax.axis_size("ctx")
    place = lax.axis_index("ctx")
    rows = block.shape[0] // count
    ring = [(i, (i + 1) % count) for i in range(count)]

    def chunk(index):
        return lax.dynamic_slice_in_dim(block, (index % count) * rows, rows, 0)

    running = chunk(place + count)
    for step in range(1, count):
        arrived = lax.ppermute(running.astype(jnp.bfloat16), "ctx", ring)
        running = arrived.astype(jnp.float32) + chunk(place + count - step)
    held = keep_low(running)
    full = jnp.zeros(block.shape, jnp.float32)
    for step in range(count):
        if step:
            held = lax.ppermute(held, "ctx", ring)
        full = lax.dynamic_update_slice_in_dim(
            full, held.astype(jnp.float32), ((place + 1 + count - step) % count) * rows, 0
        )
    return full


def everywhere(values):
    for axis in ("tp", "fsdp", "ctx"):
        step = 1
        while step < lax.axis_size(axis):
            values = values + lax.ppermute(values, axis, pairs(axis, step))
            step *= 2
    return values


def visible_keys(start_ref, place_ref, key_count):
    key_place = lax.broadcasted_iota(jnp.int32, (key_count, start_ref.shape[-1]), 0)
    return (key_place >= start_ref[0]) & (key_place <= place_ref[0])


LAST = (((1,), (1,)), ((), ()))


def attend_kernel(start_ref, place_ref, query_ref, key_ref, value_t_ref, out_ref, log_ref):
    scores = lax.dot_general(key_ref[0], query_ref[0], LAST, preferred_element_type=jnp.float32)
    scores = jnp.where(visible_keys(start_ref, place_ref, key_ref.shape[1]), scores, -1e30)
    row_max = jnp.max(scores, axis=0, keepdims=True)
    exponent = jnp.exp(scores - row_max)
    row_total = jnp.sum(exponent, axis=0, keepdims=True)
    weights_soft = (exponent * (1.0 / row_total)).astype(jnp.bfloat16)
    attended = jnp.dot(value_t_ref[0], weights_soft, preferred_element_type=jnp.float32)
    out_ref[0] = attended.T.astype(jnp.bfloat16)
    log_ref[0] = row_max + jnp.log(row_total)


def back_kernel(
    start_ref,
    place_ref,
    query_ref,
    grad_ref,
    key_ref,
    key_t_ref,
    value_ref,
    log_ref,
    grad_query_ref,
    grad_key_ref,
    grad_value_ref,
    key_total,
    value_total,
):
    tile = pl.program_id(1)

    @pl.when(tile == 0)
    def _():
        key_total[...] = jnp.zeros_like(key_total)
        value_total[...] = jnp.zeros_like(value_total)

    query = query_ref[0]
    grad = grad_ref[0]
    scores = lax.dot_general(key_ref[0], query, LAST, preferred_element_type=jnp.float32)
    scores = jnp.where(visible_keys(start_ref, place_ref, key_ref.shape[1]), scores, -1e30)
    weights_soft = jnp.exp(scores - log_ref[0])
    grad_soft = lax.dot_general(value_ref[0], grad, LAST, preferred_element_type=jnp.float32)
    delta = jnp.sum(weights_soft * grad_soft, axis=0, keepdims=True)
    grad_scores = (weights_soft * (grad_soft - delta)).astype(jnp.bfloat16)
    grad_query = jnp.dot(key_t_ref[0], grad_scores, preferred_element_type=jnp.float32)
    grad_query_ref[0] = (grad_query * HD ** (-0.5)).T.astype(jnp.bfloat16)
    key_total[...] += jnp.dot(grad_scores, query, preferred_element_type=jnp.float32)
    value_total[...] += jnp.dot(
        weights_soft.astype(jnp.bfloat16), grad, preferred_element_type=jnp.float32
    )

    @pl.when(tile == pl.num_programs(1) - 1)
    def _():
        grad_key_ref[0] = key_total[...].astype(jnp.bfloat16)
        grad_value_ref[0] = value_total[...].astype(jnp.bfloat16)


def attention_specs(groups, tok_rows, key_count, tile):
    per_token = tok_rows // tile
    row = pl.BlockSpec((1, 1, tile), lambda i, j: (i // groups, 0, j % per_token))
    query = pl.BlockSpec((1, tile, HD), lambda i, j: (i, j, 0))
    key = pl.BlockSpec((1, key_count, HD), lambda i, j: (i, 0, 0))
    key_t = pl.BlockSpec((1, HD, key_count), lambda i, j: (i, 0, 0))
    log = pl.BlockSpec((1, 1, tile), lambda i, j: (i, 0, j))
    return row, query, key, key_t, log


def cost(items, rows, key_count, dots):
    return pl.CostEstimate(
        flops=2 * dots * items * rows * key_count * HD,
        bytes_accessed=4 * items * (rows + key_count) * HD,
        transcendentals=items * rows * key_count,
    )


PARAMS = pltpu.CompilerParams(vmem_limit_bytes=50 * 1024 * 1024)


def attend(start, place, queries, keys, values_t, groups):
    items, rows, _ = queries.shape
    key_count = keys.shape[1]
    tile = min(256, start.shape[-1])
    row, query, key, key_t, log = attention_specs(groups, start.shape[-1], key_count, tile)
    return pl.pallas_call(
        attend_kernel,
        grid=(items, rows // tile),
        in_specs=[row, row, query, key, key_t],
        out_specs=[query, log],
        out_shape=[
            jax.ShapeDtypeStruct((items, rows, HD), jnp.bfloat16),
            jax.ShapeDtypeStruct((items, 1, rows), jnp.float32),
        ],
        compiler_params=PARAMS,
        cost_estimate=cost(items, rows, key_count, 2),
    )(start, place, queries, keys, values_t)


def attend_back(start, place, queries, grads, keys, keys_t, values, log_total, groups):
    items, rows, _ = queries.shape
    key_count = keys.shape[1]
    tile = min(256, start.shape[-1])
    row, query, key, key_t, log = attention_specs(groups, start.shape[-1], key_count, tile)
    return pl.pallas_call(
        back_kernel,
        grid=(items, rows // tile),
        in_specs=[row, row, query, query, key, key_t, key, log],
        out_specs=[query, key, key],
        out_shape=[
            jax.ShapeDtypeStruct((items, rows, HD), jnp.bfloat16),
            jax.ShapeDtypeStruct((items, key_count, HD), jnp.bfloat16),
            jax.ShapeDtypeStruct((items, key_count, HD), jnp.bfloat16),
        ],
        scratch_shapes=[
            pltpu.VMEM((key_count, HD), jnp.float32),
            pltpu.VMEM((key_count, HD), jnp.float32),
        ],
        compiler_params=PARAMS,
        cost_estimate=cost(items, rows, key_count, 5),
    )(start, place, queries, grads, keys, keys_t, values, log_total)


def dot_nt(left, right):
    return lax.dot_general(left, right, LAST, preferred_element_type=jnp.float32)


def dot_tn(left, right):
    return lax.dot_general(
        left, right, (((0,), (0,)), ((), ())), preferred_element_type=jnp.float32
    )


def shards(
    tokens,
    lengths,
    query_weight,
    key_weight,
    value_weight,
    out_weight,
    gate_weight,
    up_weight,
    down_weight,
    attn_gain,
    ffn_gain,
    query_gain,
    key_gain,
    out_grad,
):
    pack_count, tok_rows, width = tokens.shape
    total_rows = pack_count * tok_rows
    pack_len = tok_rows * lax.axis_size("ctx")
    offset = lax.axis_index("ctx") * tok_rows
    q_width = query_weight.shape[1]
    k_width = key_weight.shape[1]
    units = gate_weight.shape[1]
    groups = k_width // HD
    heads = q_width // HD
    per_group = heads // groups
    qkv_shard = jnp.concatenate([query_weight, key_weight, value_weight], axis=1)
    full_qkv = gather(qkv_shard, 0)
    full_out = gather(out_weight, 1)
    full_gate = gather(gate_weight, 0)
    full_up = gather(up_weight, 0)
    full_down = gather(down_weight, 1)

    local_place = offset + jnp.arange(tok_rows, dtype=jnp.int32)
    seq_ends = jnp.cumsum(lengths, axis=1)
    passed = (local_place[None, :, None] >= seq_ends[:, None, :]).astype(jnp.int32)
    local_start = jnp.sum(passed * lengths[:, None, :], axis=2)
    rope_pos = (local_place[None, :] - local_start).astype(jnp.float32)
    start_rows = local_start[:, None, :]
    place_rows = jnp.broadcast_to(local_place, (pack_count, 1, tok_rows))

    inputs = tokens.reshape(total_rows, width).astype(jnp.float32)
    cotangent = out_grad.reshape(total_rows, width)
    normed = rms_norm(inputs, attn_gain).astype(jnp.bfloat16)
    projected = jnp.dot(normed, full_qkv, preferred_element_type=jnp.float32)
    shaped = projected.reshape(pack_count, tok_rows, -1)
    query_proj = shaped[..., :q_width]
    key_proj = shaped[..., q_width : q_width + k_width]
    value_low = shaped[..., q_width + k_width :].astype(jnp.bfloat16)
    queries, query_pull = jax.vjp(
        lambda values, gain_vec: head_prep(values, gain_vec, rope_pos), query_proj, query_gain
    )
    keys_rot, key_pull = jax.vjp(
        lambda values, gain_vec: head_prep(values, gain_vec, rope_pos), key_proj, key_gain
    )
    keys_low = keys_rot.astype(jnp.bfloat16).reshape(pack_count, tok_rows, k_width)
    all_kv = lax.all_gather(
        jnp.concatenate([keys_low, value_low], axis=-1), "ctx", axis=1, tiled=True
    )
    kv_items = all_kv.reshape(pack_count, pack_len, 2, groups, HD)
    kv_items = jnp.transpose(kv_items, (2, 0, 3, 1, 4)).reshape(
        2, pack_count * groups, pack_len, HD
    )
    key_items, value_items = kv_items[0], kv_items[1]
    key_t_items = jnp.swapaxes(key_items, 1, 2)
    value_t_items = jnp.swapaxes(value_items, 1, 2)

    def to_rows(values):
        split = values.reshape(pack_count, tok_rows, groups, per_group, HD)
        return jnp.transpose(split, (0, 2, 3, 1, 4)).reshape(
            pack_count * groups, per_group * tok_rows, HD
        )

    def from_rows(values):
        split = values.reshape(pack_count, groups, per_group, tok_rows, HD)
        return jnp.transpose(split, (0, 3, 1, 2, 4)).reshape(total_rows, heads * HD)

    query_items = to_rows((queries * HD ** (-0.5)).astype(jnp.bfloat16))
    attended_items, log_total = attend(
        start_rows, place_rows, query_items, key_items, value_t_items, groups
    )
    attended = from_rows(attended_items)
    attn_part = jnp.dot(attended, full_out, preferred_element_type=jnp.float32)
    after_attn = inputs + both(attn_part)
    normed_ffn = rms_norm(after_attn, ffn_gain).astype(jnp.bfloat16)
    gate_proj = jnp.dot(normed_ffn, full_gate, preferred_element_type=jnp.float32)
    up_proj = jnp.dot(normed_ffn, full_up, preferred_element_type=jnp.float32)
    hidden, swiglu_pull = jax.vjp(
        lambda gate_in, up_in: jax.nn.silu(gate_in) * up_in, gate_proj, up_proj
    )
    hidden = hidden.astype(jnp.bfloat16)

    def columns(values, index, extent):
        return lax.dynamic_slice_in_dim(values, index * extent, extent, 1)

    down_extent = down_weight.shape[1]
    row_extent = gate_weight.shape[0]
    share_down = over_ctx(
        reduce_blocks(lambda b: dot_tn(hidden, columns(cotangent, b, down_extent)))
    )
    grad_hidden = dot_nt(cotangent, full_down)
    grad_gate_proj, grad_up_proj = swiglu_pull(grad_hidden)
    grad_gate_proj = grad_gate_proj.astype(jnp.bfloat16)
    grad_up_proj = grad_up_proj.astype(jnp.bfloat16)
    grad_normed_ffn = dot_nt(grad_gate_proj, full_gate) + dot_nt(grad_up_proj, full_up)
    unused_ffn, ffn_pull = jax.vjp(rms_norm, after_attn, ffn_gain)
    grad_after_part, grad_ffn_gain = ffn_pull(grad_normed_ffn)
    grad_after = cotangent.astype(jnp.float32) + both(grad_after_part)
    ffn_out = both(jnp.dot(hidden, full_down, preferred_element_type=jnp.float32))
    mixed = (after_attn + ffn_out).astype(jnp.bfloat16)
    share_gate = over_ctx(
        reduce_blocks(lambda b: dot_tn(columns(normed_ffn, b, row_extent), grad_gate_proj))
    )
    share_up = over_ctx(
        reduce_blocks(lambda b: dot_tn(columns(normed_ffn, b, row_extent), grad_up_proj))
    )
    grad_after_low = grad_after.astype(jnp.bfloat16)
    grad_attended = dot_nt(grad_after_low, full_out).astype(jnp.bfloat16)
    share_out = over_ctx(
        reduce_blocks(lambda b: dot_tn(attended, columns(grad_after_low, b, down_extent)))
    )
    grad_q_items, grad_k_items, grad_v_items = attend_back(
        start_rows,
        place_rows,
        query_items,
        to_rows(grad_attended),
        key_items,
        key_t_items,
        value_items,
        log_total,
        groups,
    )
    grad_kv = jnp.stack([grad_k_items, grad_v_items]).reshape(
        2, pack_count, groups, pack_len, HD
    )
    grad_kv = jnp.transpose(grad_kv, (1, 3, 0, 2, 4)).reshape(pack_count, pack_len, 2 * k_width)
    own_kv = lax.psum_scatter(grad_kv, "ctx", scatter_dimension=1, tiled=True)
    own_kv = lax.optimization_barrier(own_kv.astype(jnp.bfloat16))
    grad_keys = own_kv[..., :k_width].reshape(pack_count, tok_rows, groups, HD)
    grad_value_low = own_kv[..., k_width:].reshape(total_rows, k_width)
    grad_queries = from_rows(grad_q_items).reshape(pack_count, tok_rows, heads, HD)
    grad_query_proj, grad_query_gain = query_pull(grad_queries.astype(jnp.float32))
    grad_key_proj, grad_key_gain = key_pull(grad_keys.astype(jnp.float32))
    grad_qkv = jnp.concatenate(
        [
            grad_query_proj.astype(jnp.bfloat16).reshape(total_rows, q_width),
            grad_key_proj.astype(jnp.bfloat16).reshape(total_rows, k_width),
            grad_value_low,
        ],
        axis=1,
    )
    share_qkv = over_ctx(
        reduce_blocks(lambda b: dot_tn(columns(normed, b, row_extent), grad_qkv))
    )
    grad_normed = dot_nt(grad_qkv, full_qkv)
    unused_attn, attn_pull = jax.vjp(rms_norm, inputs, attn_gain)
    grad_input_part, grad_attn_gain = attn_pull(grad_normed)
    tokens_grad = grad_after + both(grad_input_part)
    gain_parts = (grad_attn_gain, grad_ffn_gain, grad_query_gain, grad_key_gain)
    gain_sums = everywhere(jnp.concatenate(gain_parts))
    bounds = [0]
    for part in gain_parts:
        bounds.append(bounds[-1] + part.shape[0])
    return (
        mixed.reshape(tokens.shape),
        tokens_grad.reshape(tokens.shape),
        share_qkv[:, :q_width],
        share_qkv[:, q_width : q_width + k_width],
        share_qkv[:, q_width + k_width :],
        share_out,
        share_gate,
        share_up,
        share_down,
        gain_sums[bounds[0] : bounds[1]],
        gain_sums[bounds[1] : bounds[2]],
        gain_sums[bounds[2] : bounds[3]],
        gain_sums[bounds[3] : bounds[4]],
    )


def solution(mesh):
    in_specs = (
        P("fsdp", "ctx", None),
        P("fsdp", None),
        P("fsdp", "tp"),
        P("fsdp", "tp"),
        P("fsdp", "tp"),
        P("tp", "fsdp"),
        P("fsdp", "tp"),
        P("fsdp", "tp"),
        P("tp", "fsdp"),
        P(),
        P(),
        P(),
        P(),
        P("fsdp", "ctx", None),
    )
    out_specs = (
        P("fsdp", "ctx", None),
        P("fsdp", "ctx", None),
        P("fsdp", "tp"),
        P("fsdp", "tp"),
        P("fsdp", "tp"),
        P("tp", "fsdp"),
        P("fsdp", "tp"),
        P("fsdp", "tp"),
        P("tp", "fsdp"),
        P(),
        P(),
        P(),
        P(),
    )
    return jax.shard_map(shards, mesh=mesh, in_specs=in_specs, out_specs=out_specs, check_vma=False)
```

```python
import jax
import jax.numpy as jnp
from jax import lax
from jax.experimental import pallas as pl
from jax.experimental.pallas import tpu as pltpu
from jax.sharding import PartitionSpec as P

HD = 64


EPSILON = 1e-05
ROPE_BASE = 1000000.0


def rms_norm(values, gain_vec):
    return (
        values * lax.rsqrt(jnp.mean(values * values, axis=-1, keepdims=True) + EPSILON) * gain_vec
    )


def rotate(values, rope_pos):
    half_dim = HD // 2
    frequency = ROPE_BASE ** (-2.0 * jnp.arange(half_dim, dtype=jnp.float32) / HD)
    angles = rope_pos[..., None, None] * frequency
    cosine = jnp.cos(angles)
    sine_part = jnp.sin(angles)
    lower_half = values[..., :half_dim]
    upper_half = values[..., half_dim:]
    return jnp.concatenate(
        [
            lower_half * cosine - upper_half * sine_part,
            upper_half * cosine + lower_half * sine_part,
        ],
        axis=-1,
    )


def head_prep(projected, gain_vec, rope_pos):
    shaped = projected.reshape(projected.shape[:-1] + (-1, HD))
    return rotate(rms_norm(shaped, gain_vec), rope_pos)


def pairs(axis, step):
    return [(i, i ^ step) for i in range(lax.axis_size(axis))]


def keep_low(values):
    return lax.optimization_barrier(values.astype(jnp.bfloat16))


def both(values):
    total = keep_low(values)
    step = 1
    while step < lax.axis_size("tp"):
        other = lax.ppermute(total, "tp", pairs("tp", step))
        total = total.astype(jnp.float32) + other.astype(jnp.float32)
        step *= 2
        if step < lax.axis_size("tp"):
            total = keep_low(total)
    return total.astype(jnp.float32)


def gather(shard, axis):
    count = lax.axis_size("fsdp")
    mine = lax.axis_index("fsdp")
    pieces = {0: shard}
    step = count // 2
    while step >= 1:
        moved = {
            p ^ step: lax.ppermute(piece, "fsdp", pairs("fsdp", step))
            for p, piece in pieces.items()
        }
        pieces.update(moved)
        step //= 2
    extent = shard.shape[axis]
    reps = [1, 1]
    reps[axis] = count
    full = jnp.tile(shard, reps)
    for p, piece in pieces.items():
        if p:
            full = lax.dynamic_update_slice_in_dim(full, piece, (mine ^ p) * extent, axis)
    return full


def reduce_blocks(block_of):
    count = lax.axis_size("fsdp")
    mine = lax.axis_index("fsdp")
    held = {}
    for p in sorted(range(count), key=lambda p: -(p & 1)):
        held[p] = block_of(mine ^ p)
    step = 1
    while step < count:
        sent = {
            p: lax.ppermute(block.astype(jnp.bfloat16), "fsdp", pairs("fsdp", step))
            for p, block in held.items()
            if p & step
        }
        held = {
            p: block + sent[p ^ step].astype(jnp.float32)
            for p, block in held.items()
            if not p & step
        }
        step *= 2
    return held[0]


def summed(block):
    return lax.psum(block.astype(jnp.bfloat16), "ctx").astype(jnp.float32)


def over_ctx(block):
    count = lax.axis_size("ctx")
    place = lax.axis_index("ctx")
    rows = block.shape[0] // count

    def away(shift):
        return [(i, (i + shift) % count) for i in range(count)]

    def chunk(index):
        return lax.dynamic_slice_in_dim(block, (index % count) * rows, rows, 0)

    running = chunk(place)
    for shift in range(1, count):
        sent = chunk(place + shift).astype(jnp.bfloat16)
        running = running + lax.ppermute(sent, "ctx", away(shift)).astype(jnp.float32)
    held = keep_low(running)
    full = jnp.zeros(block.shape, jnp.float32)
    for shift in range(count):
        piece = lax.ppermute(held, "ctx", away(shift)) if shift else held
        full = lax.dynamic_update_slice_in_dim(
            full, piece.astype(jnp.float32), ((place + count - shift) % count) * rows, 0
        )
    return full


def everywhere(values):
    for axis in ("tp", "fsdp", "ctx"):
        step = 1
        while step < lax.axis_size(axis):
            values = values + lax.ppermute(values, axis, pairs(axis, step))
            step *= 2
    return values


def visible_keys(start_ref, place_ref, key_count):
    key_place = lax.broadcasted_iota(jnp.int32, (key_count, start_ref.shape[-1]), 0)
    return (key_place >= start_ref[0]) & (key_place <= place_ref[0])


LAST = (((1,), (1,)), ((), ()))


def hidden_bias(start_ref, place_ref, key_count):
    return jnp.where(visible_keys(start_ref, place_ref, key_count), 0.0, -1e30)


def head(ref, at):
    return ref[0, :, at * HD : (at + 1) * HD]


def attend_kernel(start_ref, place_ref, query_ref, key_ref, value_ref, out_ref, log_ref):
    bias = hidden_bias(start_ref, place_ref, key_ref.shape[1])
    per_group = log_ref.shape[1] // 2
    results = []
    for group in range(2):
        key, value = head(key_ref, group), head(value_ref, group)
        for at in range(group * per_group, (group + 1) * per_group):
            scores = dot_nt(key, head(query_ref, at)) + bias
            row_max = jnp.max(scores, axis=0, keepdims=True)
            exponent = jnp.exp(scores - row_max)
            row_total = jnp.sum(exponent, axis=0, keepdims=True)
            attended = dot_tn(value, exponent.astype(jnp.bfloat16))
            results.append(attended * (1.0 / row_total))
            log_ref[0, at : at + 1, :] = row_max + jnp.log(row_total)
    out_ref[0] = jnp.concatenate(results, axis=0).T.astype(jnp.bfloat16)


def back_kernel(
    start_ref,
    place_ref,
    query_ref,
    grad_ref,
    key_ref,
    value_ref,
    log_ref,
    grad_query_ref,
    grad_key_ref,
    grad_value_ref,
    key_total,
    value_total,
):
    tile = pl.program_id(1)

    @pl.when(tile == 0)
    def _():
        key_total[...] = jnp.zeros_like(key_total)
        value_total[...] = jnp.zeros_like(value_total)

    bias = hidden_bias(start_ref, place_ref, key_ref.shape[1])
    per_group = log_ref.shape[1] // 2
    results = []
    for group in range(2):
        key, value = head(key_ref, group), head(value_ref, group)
        key_part, value_part = 0.0, 0.0
        for at in range(group * per_group, (group + 1) * per_group):
            query, grad = head(query_ref, at), head(grad_ref, at)
            scores = dot_nt(key, query) + bias
            weights_soft = jnp.exp(scores - log_ref[0, at : at + 1, :])
            grad_soft = dot_nt(value, grad)
            delta = jnp.sum(weights_soft * grad_soft, axis=0, keepdims=True)
            grad_scores = (weights_soft * (grad_soft - delta)).astype(jnp.bfloat16)
            results.append(dot_tn(key, grad_scores) * HD ** (-0.5))
            key_part += jnp.dot(grad_scores, query, preferred_element_type=jnp.float32)
            value_part += jnp.dot(
                weights_soft.astype(jnp.bfloat16), grad, preferred_element_type=jnp.float32
            )
        lanes = slice(group * HD, (group + 1) * HD)
        key_total[:, lanes] += key_part
        value_total[:, lanes] += value_part
    grad_query_ref[0] = jnp.concatenate(results, axis=0).T.astype(jnp.bfloat16)

    @pl.when(tile == pl.num_programs(1) - 1)
    def _():
        grad_key_ref[0] = key_total[...].astype(jnp.bfloat16)
        grad_value_ref[0] = value_total[...].astype(jnp.bfloat16)


def attention_specs(halves, per_pair, key_count, tile):
    row = pl.BlockSpec((1, 1, tile), lambda i, j: (i // halves, 0, j))
    query = pl.BlockSpec((1, tile, per_pair * HD), lambda i, j: (i // halves, j, i % halves))
    key = pl.BlockSpec((1, key_count, 2 * HD), lambda i, j: (i // halves, 0, i % halves))
    value = pl.BlockSpec((1, key_count, 2 * HD), lambda i, j: (i // halves, 0, halves + i % halves))
    log = pl.BlockSpec((1, per_pair, tile), lambda i, j: (i, 0, j))
    return row, query, key, value, log


def cost(queries, key_count, weight):
    return pl.CostEstimate(
        flops=weight * queries.size * key_count, bytes_accessed=queries.size * 8, transcendentals=0
    )


PARAMS = pltpu.CompilerParams(vmem_limit_bytes=50 * 1024 * 1024)


def attend(start, place, queries, all_kv, groups):
    packs, rows, q_width = queries.shape
    key_count = all_kv.shape[1]
    tile = min(256, rows)
    halves = groups // 2
    per_pair = q_width // HD // halves
    row, query, key, value, log = attention_specs(halves, per_pair, key_count, tile)
    return pl.pallas_call(
        attend_kernel,
        grid=(packs * halves, rows // tile),
        in_specs=[row, row, query, key, value],
        out_specs=[query, log],
        out_shape=[
            jax.ShapeDtypeStruct(queries.shape, jnp.bfloat16),
            jax.ShapeDtypeStruct((packs * halves, per_pair, rows), jnp.float32),
        ],
        compiler_params=PARAMS,
        cost_estimate=cost(queries, key_count, 50),
    )(start, place, queries, all_kv, all_kv)


def attend_back(start, place, queries, grads, all_kv, log_total, groups):
    packs, rows, q_width = queries.shape
    key_count = all_kv.shape[1]
    tile = min(256, rows)
    halves = groups // 2
    per_pair = q_width // HD // halves
    row, query, key, value, log = attention_specs(halves, per_pair, key_count, tile)
    return pl.pallas_call(
        back_kernel,
        grid=(packs * halves, rows // tile),
        in_specs=[row, row, query, query, key, value, log],
        out_specs=[query, key, key],
        out_shape=[
            jax.ShapeDtypeStruct(queries.shape, jnp.bfloat16),
            jax.ShapeDtypeStruct((packs, key_count, groups * HD), jnp.bfloat16),
            jax.ShapeDtypeStruct((packs, key_count, groups * HD), jnp.bfloat16),
        ],
        scratch_shapes=[
            pltpu.VMEM((key_count, 2 * HD), jnp.float32),
            pltpu.VMEM((key_count, 2 * HD), jnp.float32),
        ],
        compiler_params=PARAMS,
        cost_estimate=cost(queries, key_count, 80),
    )(start, place, queries, grads, all_kv, all_kv, log_total)


def dot_nt(left, right):
    return lax.dot_general(left, right, LAST, preferred_element_type=jnp.float32)


def dot_tn(left, right):
    return lax.dot_general(
        left, right, (((0,), (0,)), ((), ())), preferred_element_type=jnp.float32
    )


def shards(
    tokens,
    lengths,
    query_weight,
    key_weight,
    value_weight,
    out_weight,
    gate_weight,
    up_weight,
    down_weight,
    attn_gain,
    ffn_gain,
    query_gain,
    key_gain,
    out_grad,
):
    pack_count, tok_rows, width = tokens.shape
    total_rows = pack_count * tok_rows
    pack_len = tok_rows * lax.axis_size("ctx")
    offset = lax.axis_index("ctx") * tok_rows
    q_width = query_weight.shape[1]
    k_width = key_weight.shape[1]
    units = gate_weight.shape[1]
    groups = k_width // HD
    heads = q_width // HD
    qkv_shard = jnp.concatenate([query_weight, key_weight, value_weight], axis=1)
    full_qkv = gather(qkv_shard, 0)
    full_out = gather(out_weight, 1)
    full_gate = gather(gate_weight, 0)
    full_up = gather(up_weight, 0)
    full_down = gather(down_weight, 1)

    local_place = offset + jnp.arange(tok_rows, dtype=jnp.int32)
    seq_ends = jnp.cumsum(lengths, axis=1)
    passed = (local_place[None, :, None] >= seq_ends[:, None, :]).astype(jnp.int32)
    local_start = jnp.sum(passed * lengths[:, None, :], axis=2)
    rope_pos = (local_place[None, :] - local_start).astype(jnp.float32)
    start_rows = local_start[:, None, :]
    place_rows = jnp.broadcast_to(local_place, (pack_count, 1, tok_rows))

    inputs = tokens.reshape(total_rows, width).astype(jnp.float32)
    cotangent = out_grad.reshape(total_rows, width)
    normed = rms_norm(inputs, attn_gain).astype(jnp.bfloat16)
    projected = jnp.dot(normed, full_qkv, preferred_element_type=jnp.float32)
    shaped = projected.reshape(pack_count, tok_rows, -1)
    query_proj = shaped[..., :q_width]
    key_proj = shaped[..., q_width : q_width + k_width]
    value_low = shaped[..., q_width + k_width :].astype(jnp.bfloat16)
    queries, query_pull = jax.vjp(
        lambda values, gain_vec: head_prep(values, gain_vec, rope_pos), query_proj, query_gain
    )
    keys_rot, key_pull = jax.vjp(
        lambda values, gain_vec: head_prep(values, gain_vec, rope_pos), key_proj, key_gain
    )
    keys_low = keys_rot.astype(jnp.bfloat16).reshape(pack_count, tok_rows, k_width)
    all_kv = lax.all_gather(
        jnp.concatenate([keys_low, value_low], axis=-1), "ctx", axis=1, tiled=True
    )
    query_rows = (queries * HD ** (-0.5)).astype(jnp.bfloat16).reshape(pack_count, tok_rows, q_width)
    attended_rows, log_total = attend(start_rows, place_rows, query_rows, all_kv, groups)
    attended = attended_rows.reshape(total_rows, q_width)
    attn_part = jnp.dot(attended, full_out, preferred_element_type=jnp.float32)
    after_attn = inputs + both(attn_part)
    normed_ffn = rms_norm(after_attn, ffn_gain).astype(jnp.bfloat16)
    gate_proj = jnp.dot(normed_ffn, full_gate, preferred_element_type=jnp.float32)
    up_proj = jnp.dot(normed_ffn, full_up, preferred_element_type=jnp.float32)
    hidden, swiglu_pull = jax.vjp(
        lambda gate_in, up_in: jax.nn.silu(gate_in) * up_in, gate_proj, up_proj
    )
    hidden = hidden.astype(jnp.bfloat16)

    def columns(values, index, extent):
        return lax.dynamic_slice_in_dim(values, index * extent, extent, 1)

    down_extent = down_weight.shape[1]
    row_extent = gate_weight.shape[0]
    held_down = reduce_blocks(lambda b: dot_tn(hidden, columns(cotangent, b, down_extent)))
    held_down = held_down.astype(jnp.bfloat16)
    grad_hidden = dot_nt(cotangent, full_down)
    grad_gate_proj, grad_up_proj = swiglu_pull(grad_hidden)
    grad_gate_proj = grad_gate_proj.astype(jnp.bfloat16)
    grad_up_proj = grad_up_proj.astype(jnp.bfloat16)
    grad_normed_ffn = dot_nt(grad_gate_proj, full_gate) + dot_nt(grad_up_proj, full_up)
    unused_ffn, ffn_pull = jax.vjp(rms_norm, after_attn, ffn_gain)
    grad_after_part, grad_ffn_gain = ffn_pull(grad_normed_ffn)
    grad_after_sum, held_down = lax.optimization_barrier((both(grad_after_part), held_down))
    share_down = summed(held_down)
    grad_after = cotangent.astype(jnp.float32) + grad_after_sum
    grad_after_low = grad_after.astype(jnp.bfloat16)
    ffn_part = jnp.dot(hidden, full_down, preferred_element_type=jnp.float32)
    ffn_part, grad_after_low = lax.optimization_barrier(
        (ffn_part.astype(jnp.bfloat16), grad_after_low)
    )
    mixed = (after_attn + both(ffn_part)).astype(jnp.bfloat16)
    held_gate = reduce_blocks(lambda b: dot_tn(columns(normed_ffn, b, row_extent), grad_gate_proj))
    held_gate = held_gate.astype(jnp.bfloat16)
    held_up = reduce_blocks(lambda b: dot_tn(columns(normed_ffn, b, row_extent), grad_up_proj))
    held_up = held_up.astype(jnp.bfloat16)
    grad_attended = dot_nt(grad_after_low, full_out).astype(jnp.bfloat16)
    grad_attended, held_gate = lax.optimization_barrier((grad_attended, held_gate))
    held_gate, share_down = lax.optimization_barrier((held_gate, share_down))
    share_gate = summed(held_gate)
    share_out = over_ctx(
        reduce_blocks(lambda b: dot_tn(attended, columns(grad_after_low, b, down_extent)))
    )
    grad_q_rows, grad_k_rows, grad_v_rows = attend_back(
        start_rows,
        place_rows,
        query_rows,
        grad_attended.reshape(pack_count, tok_rows, q_width),
        all_kv,
        log_total,
        groups,
    )
    grad_kv = jnp.concatenate([grad_k_rows, grad_v_rows], axis=-1)
    grad_kv, share_gate = lax.optimization_barrier((grad_kv, share_gate))
    own_kv = lax.psum_scatter(grad_kv, "ctx", scatter_dimension=1, tiled=True)
    own_kv, held_up = lax.optimization_barrier((own_kv.astype(jnp.bfloat16), held_up))
    share_up = summed(held_up)
    grad_keys = own_kv[..., :k_width].reshape(pack_count, tok_rows, groups, HD)
    grad_value_low = own_kv[..., k_width:].reshape(total_rows, k_width)
    grad_queries = grad_q_rows.reshape(pack_count, tok_rows, heads, HD)
    grad_query_proj, grad_query_gain = query_pull(grad_queries.astype(jnp.float32))
    grad_key_proj, grad_key_gain = key_pull(grad_keys.astype(jnp.float32))
    grad_qkv = jnp.concatenate(
        [
            grad_query_proj.astype(jnp.bfloat16).reshape(total_rows, q_width),
            grad_key_proj.astype(jnp.bfloat16).reshape(total_rows, k_width),
            grad_value_low,
        ],
        axis=1,
    )
    share_qkv = over_ctx(
        reduce_blocks(lambda b: dot_tn(columns(normed, b, row_extent), grad_qkv))
    )
    grad_normed = dot_nt(grad_qkv, full_qkv)
    unused_attn, attn_pull = jax.vjp(rms_norm, inputs, attn_gain)
    grad_input_part, grad_attn_gain = attn_pull(grad_normed)
    tokens_grad = grad_after + both(grad_input_part)
    gain_parts = (grad_attn_gain, grad_ffn_gain, grad_query_gain, grad_key_gain)
    gain_sums = everywhere(jnp.concatenate(gain_parts))
    bounds = [0]
    for part in gain_parts:
        bounds.append(bounds[-1] + part.shape[0])
    return (
        mixed.reshape(tokens.shape),
        tokens_grad.reshape(tokens.shape),
        share_qkv[:, :q_width],
        share_qkv[:, q_width : q_width + k_width],
        share_qkv[:, q_width + k_width :],
        share_out,
        share_gate,
        share_up,
        share_down,
        gain_sums[bounds[0] : bounds[1]],
        gain_sums[bounds[1] : bounds[2]],
        gain_sums[bounds[2] : bounds[3]],
        gain_sums[bounds[3] : bounds[4]],
    )


def solution(mesh):
    in_specs = (
        P("fsdp", "ctx", None),
        P("fsdp", None),
        P("fsdp", "tp"),
        P("fsdp", "tp"),
        P("fsdp", "tp"),
        P("tp", "fsdp"),
        P("fsdp", "tp"),
        P("fsdp", "tp"),
        P("tp", "fsdp"),
        P(),
        P(),
        P(),
        P(),
        P("fsdp", "ctx", None),
    )
    out_specs = (
        P("fsdp", "ctx", None),
        P("fsdp", "ctx", None),
        P("fsdp", "tp"),
        P("fsdp", "tp"),
        P("fsdp", "tp"),
        P("tp", "fsdp"),
        P("fsdp", "tp"),
        P("fsdp", "tp"),
        P("tp", "fsdp"),
        P(),
        P(),
        P(),
        P(),
    )
    return jax.shard_map(shards, mesh=mesh, in_specs=in_specs, out_specs=out_specs, check_vma=False)
```

```python
import jax
import jax.numpy as jnp
from jax import lax
from jax.experimental import pallas as pl
from jax.experimental.pallas import tpu as pltpu
from jax.sharding import PartitionSpec as P

HD = 64


EPSILON = 1e-05
ROPE_BASE = 1000000.0


def rms_norm(values, gain_vec):
    return (
        values * lax.rsqrt(jnp.mean(values * values, axis=-1, keepdims=True) + EPSILON) * gain_vec
    )


def rotate(values, rope_pos):
    half_dim = HD // 2
    frequency = ROPE_BASE ** (-2.0 * jnp.arange(half_dim, dtype=jnp.float32) / HD)
    angles = rope_pos[..., None, None] * frequency
    cosine = jnp.cos(angles)
    sine_part = jnp.sin(angles)
    lower_half = values[..., :half_dim]
    upper_half = values[..., half_dim:]
    return jnp.concatenate(
        [
            lower_half * cosine - upper_half * sine_part,
            upper_half * cosine + lower_half * sine_part,
        ],
        axis=-1,
    )


def head_prep(projected, gain_vec, rope_pos):
    shaped = projected.reshape(projected.shape[:-1] + (-1, HD))
    return rotate(rms_norm(shaped, gain_vec), rope_pos)


def pairs(axis, step):
    return [(i, i ^ step) for i in range(lax.axis_size(axis))]


def keep_low(values):
    return lax.optimization_barrier(values.astype(jnp.bfloat16))


def both(values):
    total = keep_low(values)
    step = 1
    while step < lax.axis_size("tp"):
        other = lax.ppermute(total, "tp", pairs("tp", step))
        total = total.astype(jnp.float32) + other.astype(jnp.float32)
        step *= 2
        if step < lax.axis_size("tp"):
            total = keep_low(total)
    return total.astype(jnp.float32)


def fetch(shard):
    count = lax.axis_size("fsdp")
    pieces = {0: shard}
    step = count // 2
    while step >= 1:
        moved = {
            p ^ step: lax.ppermute(piece, "fsdp", pairs("fsdp", step))
            for p, piece in pieces.items()
        }
        pieces.update(moved)
        step //= 2
    return pieces


def whole(pieces, axis):
    mine = lax.axis_index("fsdp")
    shard = pieces[0]
    extent = shard.shape[axis]
    reps = [1, 1]
    reps[axis] = len(pieces)
    full = jnp.tile(shard, reps)
    for p, piece in pieces.items():
        if p:
            full = lax.dynamic_update_slice_in_dim(full, piece, (mine ^ p) * extent, axis)
    return full


def reduce_blocks(block_of):
    count = lax.axis_size("fsdp")
    mine = lax.axis_index("fsdp")
    held = {}
    for p in sorted(range(count), key=lambda p: -(p & 1)):
        held[p] = block_of(mine ^ p)
    step = 1
    while step < count:
        sent = {
            p: lax.ppermute(block.astype(jnp.bfloat16), "fsdp", pairs("fsdp", step))
            for p, block in held.items()
            if p & step
        }
        held = {
            p: block + sent[p ^ step].astype(jnp.float32)
            for p, block in held.items()
            if not p & step
        }
        step *= 2
    return held[0]


def over_ctx(block):
    count = lax.axis_size("ctx")
    place = lax.axis_index("ctx")
    rows = block.shape[0] // count

    def away(shift):
        return [(i, (i + shift) % count) for i in range(count)]

    def chunk(index):
        return lax.dynamic_slice_in_dim(block, (index % count) * rows, rows, 0)

    running = chunk(place)
    for shift in range(1, count):
        sent = chunk(place + shift).astype(jnp.bfloat16)
        running = running + lax.ppermute(sent, "ctx", away(shift)).astype(jnp.float32)
    held = keep_low(running)
    full = jnp.zeros(block.shape, jnp.float32)
    for shift in range(count):
        piece = lax.ppermute(held, "ctx", away(shift)) if shift else held
        full = lax.dynamic_update_slice_in_dim(
            full, piece.astype(jnp.float32), ((place + count - shift) % count) * rows, 0
        )
    return full


def ring_reduce(block):
    count = lax.axis_size("ctx")
    place = lax.axis_index("ctx")
    rows = block.shape[0] // count
    ring = [(i, (i + 1) % count) for i in range(count)]

    def chunk(index):
        return lax.dynamic_slice_in_dim(block, (index % count) * rows, rows, 0)

    running = chunk(place)
    for step in range(1, count):
        arrived = lax.ppermute(running.astype(jnp.bfloat16), "ctx", ring)
        running = arrived.astype(jnp.float32) + chunk(place + count - step)
    return keep_low(running)


def ring_spread(held):
    count = lax.axis_size("ctx")
    place = lax.axis_index("ctx")
    rows = held.shape[0]
    ring = [(i, (i + 1) % count) for i in range(count)]
    full = jnp.zeros((rows * count, held.shape[1]), jnp.float32)
    for step in range(count):
        if step:
            held = lax.ppermute(held, "ctx", ring)
        full = lax.dynamic_update_slice_in_dim(
            full, held.astype(jnp.float32), ((place + 1 + count - step) % count) * rows, 0
        )
    return full


def everywhere(values):
    for axis in ("tp", "fsdp", "ctx"):
        step = 1
        while step < lax.axis_size(axis):
            values = values + lax.ppermute(values, axis, pairs(axis, step))
            step *= 2
    return values


def visible_keys(start_ref, place_ref, key_count):
    key_place = lax.broadcasted_iota(jnp.int32, (key_count, start_ref.shape[-1]), 0)
    return (key_place >= start_ref[0]) & (key_place <= place_ref[0])


LAST = (((1,), (1,)), ((), ()))


def hidden_bias(start_ref, place_ref, key_count):
    return jnp.where(visible_keys(start_ref, place_ref, key_count), 0.0, -1e30)


def head(ref, at):
    return ref[0, :, at * HD : (at + 1) * HD]


def attend_kernel(start_ref, place_ref, query_ref, key_ref, value_ref, out_ref, log_ref):
    bias = hidden_bias(start_ref, place_ref, key_ref.shape[1])
    per_group = log_ref.shape[1] // 2
    results = []
    for group in range(2):
        key, value = head(key_ref, group), head(value_ref, group)
        for at in range(group * per_group, (group + 1) * per_group):
            scores = dot_nt(key, head(query_ref, at)) + bias
            row_max = jnp.max(scores, axis=0, keepdims=True)
            exponent = jnp.exp(scores - row_max)
            row_total = jnp.sum(exponent, axis=0, keepdims=True)
            attended = dot_tn(value, exponent.astype(jnp.bfloat16))
            results.append(attended * (1.0 / row_total))
            log_ref[0, at : at + 1, :] = row_max + jnp.log(row_total)
    out_ref[0] = jnp.concatenate(results, axis=0).T.astype(jnp.bfloat16)


def back_kernel(
    start_ref,
    place_ref,
    query_ref,
    grad_ref,
    key_ref,
    value_ref,
    log_ref,
    grad_query_ref,
    grad_key_ref,
    grad_value_ref,
    key_total,
    value_total,
):
    tile = pl.program_id(1)

    @pl.when(tile == 0)
    def _():
        key_total[...] = jnp.zeros_like(key_total)
        value_total[...] = jnp.zeros_like(value_total)

    bias = hidden_bias(start_ref, place_ref, key_ref.shape[1])
    per_group = log_ref.shape[1] // 2
    results = []
    for group in range(2):
        key, value = head(key_ref, group), head(value_ref, group)
        key_part, value_part = 0.0, 0.0
        for at in range(group * per_group, (group + 1) * per_group):
            query, grad = head(query_ref, at), head(grad_ref, at)
            scores = dot_nt(key, query) + bias
            weights_soft = jnp.exp(scores - log_ref[0, at : at + 1, :])
            grad_soft = dot_nt(value, grad)
            delta = jnp.sum(weights_soft * grad_soft, axis=0, keepdims=True)
            grad_scores = (weights_soft * (grad_soft - delta)).astype(jnp.bfloat16)
            results.append(dot_tn(key, grad_scores) * HD ** (-0.5))
            key_part += jnp.dot(grad_scores, query, preferred_element_type=jnp.float32)
            value_part += jnp.dot(
                weights_soft.astype(jnp.bfloat16), grad, preferred_element_type=jnp.float32
            )
        lanes = slice(group * HD, (group + 1) * HD)
        key_total[:, lanes] += key_part
        value_total[:, lanes] += value_part
    grad_query_ref[0] = jnp.concatenate(results, axis=0).T.astype(jnp.bfloat16)

    @pl.when(tile == pl.num_programs(1) - 1)
    def _():
        grad_key_ref[0] = key_total[...].astype(jnp.bfloat16)
        grad_value_ref[0] = value_total[...].astype(jnp.bfloat16)


def attention_specs(halves, per_pair, key_count, tile):
    row = pl.BlockSpec((1, 1, tile), lambda i, j: (i // halves, 0, j))
    query = pl.BlockSpec((1, tile, per_pair * HD), lambda i, j: (i // halves, j, i % halves))
    key = pl.BlockSpec((1, key_count, 2 * HD), lambda i, j: (i // halves, 0, i % halves))
    value = pl.BlockSpec((1, key_count, 2 * HD), lambda i, j: (i // halves, 0, halves + i % halves))
    log = pl.BlockSpec((1, per_pair, tile), lambda i, j: (i, 0, j))
    return row, query, key, value, log


def cost(queries, key_count, weight):
    return pl.CostEstimate(
        flops=weight * queries.size * key_count, bytes_accessed=queries.size * 8, transcendentals=0
    )


PARAMS = pltpu.CompilerParams(vmem_limit_bytes=50 * 1024 * 1024)


def attend(start, place, queries, all_kv, groups):
    packs, rows, q_width = queries.shape
    key_count = all_kv.shape[1]
    tile = min(256, rows)
    halves = groups // 2
    per_pair = q_width // HD // halves
    row, query, key, value, log = attention_specs(halves, per_pair, key_count, tile)
    return pl.pallas_call(
        attend_kernel,
        grid=(packs * halves, rows // tile),
        in_specs=[row, row, query, key, value],
        out_specs=[query, log],
        out_shape=[
            jax.ShapeDtypeStruct(queries.shape, jnp.bfloat16),
            jax.ShapeDtypeStruct((packs * halves, per_pair, rows), jnp.float32),
        ],
        compiler_params=PARAMS,
        cost_estimate=cost(queries, key_count, 50),
    )(start, place, queries, all_kv, all_kv)


def attend_back(start, place, queries, grads, all_kv, log_total, groups):
    packs, rows, q_width = queries.shape
    key_count = all_kv.shape[1]
    tile = min(256, rows)
    halves = groups // 2
    per_pair = q_width // HD // halves
    row, query, key, value, log = attention_specs(halves, per_pair, key_count, tile)
    return pl.pallas_call(
        back_kernel,
        grid=(packs * halves, rows // tile),
        in_specs=[row, row, query, query, key, value, log],
        out_specs=[query, key, key],
        out_shape=[
            jax.ShapeDtypeStruct(queries.shape, jnp.bfloat16),
            jax.ShapeDtypeStruct((packs, key_count, groups * HD), jnp.bfloat16),
            jax.ShapeDtypeStruct((packs, key_count, groups * HD), jnp.bfloat16),
        ],
        scratch_shapes=[
            pltpu.VMEM((key_count, 2 * HD), jnp.float32),
            pltpu.VMEM((key_count, 2 * HD), jnp.float32),
        ],
        compiler_params=PARAMS,
        cost_estimate=cost(queries, key_count, 80),
    )(start, place, queries, grads, all_kv, all_kv, log_total)


def dot_nt(left, right):
    return lax.dot_general(left, right, LAST, preferred_element_type=jnp.float32)


def dot_tn(left, right):
    return lax.dot_general(
        left, right, (((0,), (0,)), ((), ())), preferred_element_type=jnp.float32
    )


def shards(
    tokens,
    lengths,
    query_weight,
    key_weight,
    value_weight,
    out_weight,
    gate_weight,
    up_weight,
    down_weight,
    attn_gain,
    ffn_gain,
    query_gain,
    key_gain,
    out_grad,
):
    pack_count, tok_rows, width = tokens.shape
    total_rows = pack_count * tok_rows
    pack_len = tok_rows * lax.axis_size("ctx")
    offset = lax.axis_index("ctx") * tok_rows
    q_width = query_weight.shape[1]
    k_width = key_weight.shape[1]
    units = gate_weight.shape[1]
    groups = k_width // HD
    heads = q_width // HD
    qkv_shard = jnp.concatenate([query_weight, key_weight, value_weight], axis=1)
    full_qkv = whole(fetch(qkv_shard), 0)
    full_out = whole(fetch(out_weight), 1)
    full_gate = whole(fetch(gate_weight), 0)
    up_pieces = fetch(up_weight)
    down_pieces = fetch(down_weight)

    local_place = offset + jnp.arange(tok_rows, dtype=jnp.int32)
    seq_ends = jnp.cumsum(lengths, axis=1)
    passed = (local_place[None, :, None] >= seq_ends[:, None, :]).astype(jnp.int32)
    local_start = jnp.sum(passed * lengths[:, None, :], axis=2)
    rope_pos = (local_place[None, :] - local_start).astype(jnp.float32)
    start_rows = local_start[:, None, :]
    place_rows = jnp.broadcast_to(local_place, (pack_count, 1, tok_rows))

    inputs = tokens.reshape(total_rows, width).astype(jnp.float32)
    cotangent = out_grad.reshape(total_rows, width)
    normed = rms_norm(inputs, attn_gain).astype(jnp.bfloat16)
    projected = jnp.dot(normed, full_qkv, preferred_element_type=jnp.float32)
    shaped = projected.reshape(pack_count, tok_rows, -1)
    query_proj = shaped[..., :q_width]
    key_proj = shaped[..., q_width : q_width + k_width]
    value_low = shaped[..., q_width + k_width :].astype(jnp.bfloat16)
    queries, query_pull = jax.vjp(
        lambda values, gain_vec: head_prep(values, gain_vec, rope_pos), query_proj, query_gain
    )
    keys_rot, key_pull = jax.vjp(
        lambda values, gain_vec: head_prep(values, gain_vec, rope_pos), key_proj, key_gain
    )
    keys_low = keys_rot.astype(jnp.bfloat16).reshape(pack_count, tok_rows, k_width)
    all_kv = lax.all_gather(
        jnp.concatenate([keys_low, value_low], axis=-1), "ctx", axis=1, tiled=True
    )
    query_rows = (queries * HD ** (-0.5)).astype(jnp.bfloat16).reshape(pack_count, tok_rows, q_width)
    attended_rows, log_total = attend(start_rows, place_rows, query_rows, all_kv, groups)
    attended_rows, up_pieces, down_pieces = lax.optimization_barrier(
        (attended_rows, up_pieces, down_pieces)
    )
    full_up = whole(up_pieces, 0)
    full_down = whole(down_pieces, 1)
    attended = attended_rows.reshape(total_rows, q_width)
    attn_part = jnp.dot(attended, full_out, preferred_element_type=jnp.float32)
    after_attn = inputs + both(attn_part)
    normed_ffn = rms_norm(after_attn, ffn_gain).astype(jnp.bfloat16)
    gate_proj = jnp.dot(normed_ffn, full_gate, preferred_element_type=jnp.float32)
    up_proj = jnp.dot(normed_ffn, full_up, preferred_element_type=jnp.float32)
    hidden, swiglu_pull = jax.vjp(
        lambda gate_in, up_in: jax.nn.silu(gate_in) * up_in, gate_proj, up_proj
    )
    hidden = hidden.astype(jnp.bfloat16)

    def columns(values, index, extent):
        return lax.dynamic_slice_in_dim(values, index * extent, extent, 1)

    down_extent = down_weight.shape[1]
    row_extent = gate_weight.shape[0]
    held_down = reduce_blocks(lambda b: dot_tn(hidden, columns(cotangent, b, down_extent)))
    held_down = held_down.astype(jnp.bfloat16)
    grad_hidden = dot_nt(cotangent, full_down)
    grad_gate_proj, grad_up_proj = swiglu_pull(grad_hidden)
    grad_gate_proj = grad_gate_proj.astype(jnp.bfloat16)
    grad_up_proj = grad_up_proj.astype(jnp.bfloat16)
    grad_normed_ffn = dot_nt(grad_gate_proj, full_gate) + dot_nt(grad_up_proj, full_up)
    unused_ffn, ffn_pull = jax.vjp(rms_norm, after_attn, ffn_gain)
    grad_after_part, grad_ffn_gain = ffn_pull(grad_normed_ffn)
    grad_after_sum, held_down = lax.optimization_barrier((both(grad_after_part), held_down))
    sum_down = ring_reduce(held_down)
    grad_after = cotangent.astype(jnp.float32) + grad_after_sum
    grad_after_low = grad_after.astype(jnp.bfloat16)
    ffn_part = jnp.dot(hidden, full_down, preferred_element_type=jnp.float32)
    ffn_part, grad_after_low = lax.optimization_barrier(
        (ffn_part.astype(jnp.bfloat16), grad_after_low)
    )
    mixed = (after_attn + both(ffn_part)).astype(jnp.bfloat16)
    held_gate = reduce_blocks(lambda b: dot_tn(columns(normed_ffn, b, row_extent), grad_gate_proj))
    held_gate = held_gate.astype(jnp.bfloat16)
    held_up = reduce_blocks(lambda b: dot_tn(columns(normed_ffn, b, row_extent), grad_up_proj))
    held_up = held_up.astype(jnp.bfloat16)
    grad_attended = dot_nt(grad_after_low, full_out).astype(jnp.bfloat16)
    share_out = over_ctx(
        reduce_blocks(lambda b: dot_tn(attended, columns(grad_after_low, b, down_extent)))
    )
    grad_q_rows, grad_k_rows, grad_v_rows = attend_back(
        start_rows,
        place_rows,
        query_rows,
        grad_attended.reshape(pack_count, tok_rows, q_width),
        all_kv,
        log_total,
        groups,
    )
    grad_kv = jnp.concatenate([grad_k_rows, grad_v_rows], axis=-1)
    own_kv = lax.psum_scatter(grad_kv, "ctx", scatter_dimension=1, tiled=True)
    own_kv, sum_down, held_gate, held_up = lax.optimization_barrier(
        (own_kv.astype(jnp.bfloat16), sum_down, held_gate, held_up)
    )
    share_down = ring_spread(sum_down)
    share_gate = ring_spread(ring_reduce(held_gate))
    share_up = ring_spread(ring_reduce(held_up))
    grad_keys = own_kv[..., :k_width].reshape(pack_count, tok_rows, groups, HD)
    grad_value_low = own_kv[..., k_width:].reshape(total_rows, k_width)
    grad_queries = grad_q_rows.reshape(pack_count, tok_rows, heads, HD)
    grad_query_proj, grad_query_gain = query_pull(grad_queries.astype(jnp.float32))
    grad_key_proj, grad_key_gain = key_pull(grad_keys.astype(jnp.float32))
    grad_qkv = jnp.concatenate(
        [
            grad_query_proj.astype(jnp.bfloat16).reshape(total_rows, q_width),
            grad_key_proj.astype(jnp.bfloat16).reshape(total_rows, k_width),
            grad_value_low,
        ],
        axis=1,
    )
    share_qkv = over_ctx(
        reduce_blocks(lambda b: dot_tn(columns(normed, b, row_extent), grad_qkv))
    )
    grad_normed = dot_nt(grad_qkv, full_qkv)
    unused_attn, attn_pull = jax.vjp(rms_norm, inputs, attn_gain)
    grad_input_part, grad_attn_gain = attn_pull(grad_normed)
    tokens_grad = grad_after + both(grad_input_part)
    gain_parts = (grad_attn_gain, grad_ffn_gain, grad_query_gain, grad_key_gain)
    gain_sums = everywhere(jnp.concatenate(gain_parts))
    bounds = [0]
    for part in gain_parts:
        bounds.append(bounds[-1] + part.shape[0])
    return (
        mixed.reshape(tokens.shape),
        tokens_grad.reshape(tokens.shape),
        share_qkv[:, :q_width],
        share_qkv[:, q_width : q_width + k_width],
        share_qkv[:, q_width + k_width :],
        share_out,
        share_gate,
        share_up,
        share_down,
        gain_sums[bounds[0] : bounds[1]],
        gain_sums[bounds[1] : bounds[2]],
        gain_sums[bounds[2] : bounds[3]],
        gain_sums[bounds[3] : bounds[4]],
    )


def solution(mesh):
    in_specs = (
        P("fsdp", "ctx", None),
        P("fsdp", None),
        P("fsdp", "tp"),
        P("fsdp", "tp"),
        P("fsdp", "tp"),
        P("tp", "fsdp"),
        P("fsdp", "tp"),
        P("fsdp", "tp"),
        P("tp", "fsdp"),
        P(),
        P(),
        P(),
        P(),
        P("fsdp", "ctx", None),
    )
    out_specs = (
        P("fsdp", "ctx", None),
        P("fsdp", "ctx", None),
        P("fsdp", "tp"),
        P("fsdp", "tp"),
        P("fsdp", "tp"),
        P("tp", "fsdp"),
        P("fsdp", "tp"),
        P("fsdp", "tp"),
        P("tp", "fsdp"),
        P(),
        P(),
        P(),
        P(),
    )
    return jax.shard_map(shards, mesh=mesh, in_specs=in_specs, out_specs=out_specs, check_vma=False)
```
